256 devices in a mesh: tm: 8 (over y, z_lo), col: 32 (over x, z_hi, core).
Axes of the slice: x: 4, y: 4, z: 8 (z_hi: 4, z_lo: 2; z = z_hi * 2 + z_lo), core: 2. Of those that a mesh axis runs over, the one named last changes fastest.
Arguments:
- visibilities: float32 [64, 32, 2, 2048], P('tm', 'col'), may hold values from -6 to 6
- coords: float32 [64, 32, 2, 2048], P('tm', 'col'), may hold values from 3 to 124
- tile_row: int32 [64, 32], P('tm', 'col'), may hold values from 0 to 15
- counts: int32 [8, 32], P('tm', 'col'), may hold values from 1 to 8, as said below
- w_plane: float32 [1], replicated, may hold values from 20 to 60
Outputs:
- image_real: float32 [2048, 4096], P('tm', 'col')
- image_imag: float32 [2048, 4096], P('tm', 'col')
The draws below stay inside these ranges and needn't reach their ends.
Inputs may be any that keep to these rules, and one draw needn't show every extreme that they name: `counts`: slots of a device from its count on carry no used blocks; in every draw one device uses all 8 slots.
All inputs are finite; a program needn't handle non-finite values.
Results may differ from the reference program's by a relative error of at most 0.01.
Values sent between devices are 32-bit elements; how exact they have to be, the bound alone decides.
No kernel may reach another device: no remote copies, remote signals or barrier semaphores. Data moves between devices by JAX's collectives and lax.ppermute only.
A program may use at most 320 MiB of HBM per device.

```python
import math
import jax
import jax.numpy as jnp
from jax import lax

TILE = 128
TROWS = 16
BLK = 2048
NB = 8
BLOCKS = 64
NU = 2048
NV = 4096
N_TM = 8
N_COL = 32


def draw_counts(key, part):
    base = jax.random.randint(jax.random.fold_in(key, 11), (N_TM, N_COL), 1, NB // 2 + 1)
    chosen = jax.random.randint(jax.random.fold_in(key, 12), (), 0, N_TM * N_COL)
    flat = base.reshape(N_TM * N_COL)
    flat = jnp.where(jnp.arange(N_TM * N_COL) == chosen, NB, flat)
    return flat.reshape(N_TM, N_COL).astype(jnp.int32)


def set_ends(array, own_key, smallest, high):
    extent = array.shape
    index_at = [jax.random.randint(jax.random.fold_in(own_key, axis), (), 0, extent[axis]) for axis in range(len(extent))]
    array = array.at[tuple(index_at)].set(smallest)
    longest = extent.index(max(extent))
    index_at[longest] = (index_at[longest] + 1) % extent[longest]
    return array.at[tuple(index_at)].set(high)


def levels(own_key, dims, cuts, least, largest):
    factor_of, own = 1.0, jax.random.fold_in(own_key, 6)
    for dim, blocks in cuts:
        steps = jnp.exp(jax.random.uniform(jax.random.fold_in(own, dim), (blocks,), jnp.float32, least / len(cuts), largest / len(cuts)))
        factor_of = factor_of * jnp.repeat(steps, dims[dim] // blocks).reshape([-1 if axis == dim else 1 for axis in range(len(dims))])
    return factor_of


def noise(stream_key, dims, width, reach, cuts=(), held_as=jnp.bfloat16):
    values = jax.random.normal(stream_key, dims, jnp.float32) * width
    if len(cuts) > 0:
        values = levels(stream_key, dims, cuts, -0.22, 0.18) * values
    return jnp.clip(values, min=-reach, max=reach).astype(held_as)


def setup_inputs(seed: int = 0) -> dict:
    seeds = jax.random.split(jax.random.key(seed), 6)
    return {
        "visibilities": noise(seeds[0], (BLOCKS, N_COL, 2, BLK), 1.0, 6.0, ((0, 8), (1, 32)), jnp.float32),
        "coords": jnp.clip(3.0 + 121.0 * jax.random.uniform(seeds[1], (BLOCKS, N_COL, 2, BLK), jnp.float32) ** levels(seeds[1], (BLOCKS, N_COL, 2, BLK), ((0, 8), (1, 32)), -0.2, 0.2), 3.0, 124.0),
        "tile_row": set_ends(jax.random.randint(seeds[2], (BLOCKS, N_COL), 0, TROWS), jax.random.fold_in(seeds[2], 1), 0, TROWS - 1).astype(jnp.int32),
        "counts": draw_counts(jax.random.fold_in(seeds[5], 71), 0),
        "w_plane": jnp.clip(jax.random.uniform(seeds[4], (1,), jnp.float32, 20.0, 60.0), 20.0, 60.0),
    }


kernel_radius = 1.0
highest = lax.Precision.HIGHEST

def taper(position, cells):
    offset = cells[None, None, :] - position[:, :, None]
    inside = 1.0 - offset * offset / (kernel_radius * kernel_radius)
    inside = jnp.maximum(inside, 0.0)
    return inside * inside

def trig_table(first, second, length):
    product = first[:, None] * second[None, :] % length
    angle = product.astype(jnp.float32) * (2.0 * math.pi / length)
    return (jnp.cos(angle), jnp.sin(angle))

def matmul(left, right):
    return jnp.dot(left, right, precision=highest, preferred_element_type=jnp.float32)

def w_correct(real_image, imaginary_image, x_index, y_index, plane_depth, size_u, size_v):
    along_l = (x_index - size_u // 2).astype(jnp.float32) / size_u
    along_m = (y_index - size_v // 2).astype(jnp.float32) / size_v
    height = jnp.sqrt(1.0 - along_l[:, None] * along_l[:, None] - along_m[None, :] * along_m[None, :])
    phase = 2.0 * math.pi * plane_depth * (height - 1.0)
    cosine = jnp.cos(phase)
    sine_part = jnp.sin(phase)
    scale = 1.0 / math.sqrt(size_u * size_v)
    real_out = (real_image * cosine - imaginary_image * sine_part) * scale
    imaginary_out = (real_image * sine_part + imaginary_image * cosine) * scale
    return (real_out, imaginary_out)

def reference(visibilities, coords, tile_row, counts, w_plane):
    cells = jnp.arange(TILE, dtype=jnp.int32).astype(jnp.float32)
    block_index = jnp.arange(NB * N_TM, dtype=jnp.int32)
    owners = counts[block_index // NB, :]
    alive = (block_index % NB)[:, None] < owners

    def place(column_grid, piece, tile_index):
        corner = (tile_index * TILE).astype(jnp.int32)
        anchor = jnp.zeros((), jnp.int32)
        current = lax.dynamic_slice(column_grid, (anchor, anchor, corner), (TILE, 2, TILE))
        return lax.dynamic_update_slice(column_grid, current + piece, (anchor, anchor, corner))

    def deposit(grid, item):
        values, places, tile_rows, living = item
        weight_u = taper(places[:, 0, :], cells).astype(jnp.bfloat16)
        weight_v = taper(places[:, 1, :], cells).astype(jnp.bfloat16)
        weighted = values[:, :, :, None] * weight_u[:, None, :, :].astype(jnp.float32)
        weighted = jnp.where(living[:, None, None, None], weighted, 0.0).astype(jnp.bfloat16)
        partial_tile = jnp.einsum('ckj,cpki->cjpi', weight_v.astype(jnp.float32), weighted.astype(jnp.float32), precision=highest)
        return (jax.vmap(place)(grid, partial_tile, tile_rows), None)
    start_grid = jnp.zeros((N_COL, TILE, 2, NU), jnp.float32)
    grid, unused = lax.scan(deposit, start_grid, (visibilities, coords, tile_row, alive))
    real_grid = grid[:, :, 0, :].reshape(NV, NU).T
    imaginary_grid = grid[:, :, 1, :].reshape(NV, NU).T
    v_index = jnp.arange(NV, dtype=jnp.int32)
    cos_v, sin_v = trig_table(v_index, v_index, NV)
    real_rows = matmul(real_grid, cos_v) - matmul(imaginary_grid, sin_v)
    imaginary_rows = matmul(real_grid, sin_v) + matmul(imaginary_grid, cos_v)
    u_index = jnp.arange(NU, dtype=jnp.int32)
    cos_u, sin_u = trig_table(u_index, u_index, NU)
    real_image = matmul(cos_u, real_rows) - matmul(sin_u, imaginary_rows)
    imaginary_image = matmul(cos_u, imaginary_rows) + matmul(sin_u, real_rows)
    real_out, imaginary_out = w_correct(real_image, imaginary_image, u_index, v_index, w_plane[0], NU, NV)
    return (real_out, imaginary_out)
```

```python
import math

import jax
import jax.numpy as jnp
import numpy as np
from jax import lax
from jax.experimental import pallas as pl
from jax.experimental.pallas import tpu as pltpu
from jax.sharding import PartitionSpec as P

TILE = 128
TROWS = 16
NU = 2048
NV = 4096
GROUPS = 8
COLUMNS = 32
SLOTS = 8
BLOCK = 2048
PART = TILE // GROUPS
CHUNK = 512

f32 = jnp.float32
bf16 = jnp.bfloat16
NT = (((1,), (1,)), ((), ()))
NN = (((1,), (0,)), ((), ()))


def unit(product, length):
    angle = np.mod(product, length) * (2.0 * math.pi / length)
    return np.cos(angle), np.sin(angle)


def split(table):
    table = np.asarray(table, np.float32)
    high = table.astype(jnp.bfloat16)
    low = (table - high.astype(np.float32)).astype(jnp.bfloat16)
    return np.stack([high, low])


def inner_u_table():
    x2 = np.arange(TILE)[:, None]
    i = np.arange(TILE)[None, :]
    c, s = unit(x2 * i, TILE)
    return split(np.block([[c, -s], [s, c]]))


def twiddle_u_table():
    x1 = np.arange(TROWS)[:, None]
    i = np.arange(TILE)[None, :]
    c, s = unit(x1 * i, NU)
    return np.stack([c, s], 1).astype(np.float32)


def column_table():
    y1 = np.arange(COLUMNS)[:, None]
    c = np.arange(COLUMNS)[None, :]
    tables = []
    for g in range(GROUPS):
        co, si = unit(TILE * c * y1 + PART * g * y1, NV)
        t = np.zeros((2, COLUMNS, COLUMNS, 2))
        t[0, :, :, 0], t[0, :, :, 1] = co, -si
        t[1, :, :, 0], t[1, :, :, 1] = si, co
        tables.append(t.reshape(2 * COLUMNS, 2 * COLUMNS))
    return split(np.stack(tables))


def twiddle_v_table():
    ya = np.arange(GROUPS)[:, None, None]
    y1 = np.arange(COLUMNS)[None, :, None]
    j = (np.arange(TILE) % PART)[None, None, :]
    c, s = unit(j * (y1 + COLUMNS * ya), NV)
    return np.stack([c, s], 1).astype(np.float32)


def inner_v_table():
    yb = np.arange(PART)[:, None]
    j = np.arange(PART)[None, :]
    c, s = unit(yb * j, PART)
    t = np.zeros((PART, 2, 8, 2, 8, PART))
    for xx in range(8):
        t[:, 0, xx, 0, xx, :] = c
        t[:, 0, xx, 1, xx, :] = -s
        t[:, 1, xx, 0, xx, :] = s
        t[:, 1, xx, 1, xx, :] = c
    return split(t.reshape(256, 256))


def dot3(a_high, a_low, b, dims):
    b_high = b.astype(bf16)
    b_low = (b - b_high.astype(f32)).astype(bf16)
    def dot(x, y):
        return lax.dot_general(x, y, dims, preferred_element_type=f32)
    return dot(a_high, b_high) + (dot(a_low, b_high) + dot(a_high, b_low))


def fft(items):
    n = len(items)
    if n == 1:
        return items
    even = fft(items[0::2])
    odd = fft(items[1::2])
    out = [None] * n
    for k in range(n // 2):
        er, ei = even[k]
        a, b = odd[k]
        if k == 0:
            tr, ti = a, b
        elif 4 * k == n:
            tr, ti = -b, a
        elif 8 * k == n:
            h = math.sqrt(0.5)
            tr, ti = (a - b) * h, (a + b) * h
        elif 8 * k == 3 * n:
            h = math.sqrt(0.5)
            tr, ti = (a + b) * -h, (a - b) * h
        else:
            c, s = math.cos(2 * math.pi * k / n), math.sin(2 * math.pi * k / n)
            tr, ti = a * c - b * s, a * s + b * c
        out[k] = (er + tr, ei + ti)
        out[k + n // 2] = (er - tr, ei - ti)
    return out


def grid_kernel(count_ref, row_ref, vis_ref, place_ref, out_ref):
    count = count_ref[0, 0]
    cells = lax.broadcasted_iota(jnp.int32, (TILE, CHUNK), 0).astype(f32)

    def taper(position):
        offset = cells - position
        inside = jnp.maximum(1.0 - offset * offset, 0.0)
        return (inside * inside).astype(bf16)

    def one_slot(slot, carry):
        total = jnp.zeros((TILE, 2 * TILE), f32)
        for start in range(0, BLOCK, CHUNK):
            at = pl.ds(start, CHUNK)
            weight_u = taper(place_ref[slot, 0, 0:1, at]).astype(f32)
            weight_v = taper(place_ref[slot, 0, 1:2, at])
            real = (weight_u * vis_ref[slot, 0, 0:1, at]).astype(bf16)
            imaginary = (weight_u * vis_ref[slot, 0, 1:2, at]).astype(bf16)
            weighted = jnp.concatenate([real, imaginary], 0)
            total += lax.dot_general(weight_v, weighted, NT, preferred_element_type=f32)
        for part in range(2):
            piece = total[:, part * TILE : (part + 1) * TILE].reshape(GROUPS, PART, TILE)
            first = pl.multiple_of(slot * (2 * PART) + part * PART, PART)
            out_ref[:, pl.ds(first, PART), :] = piece
        return carry

    lax.fori_loop(0, count, one_slot, 0)
    slot_of = lax.broadcasted_iota(jnp.int32, (SLOTS, TILE), 0)
    label = jnp.full((SLOTS, TILE), TROWS, jnp.int32)
    for slot in range(SLOTS):
        here = jnp.where(slot < count, row_ref[slot, 0], TROWS)
        label = jnp.where(slot_of == slot, here, label)
    label = label.astype(f32)
    for g in range(GROUPS):
        out_ref[g, 2 * PART * SLOTS :, :] = label


def transform_u_kernel(label_ref, piece_ref, table_ref, twiddle_ref, out_ref, grid_ref, rows_ref):
    grid_ref[...] = jnp.zeros_like(grid_ref)
    for t in range(GROUPS):
        for slot in range(SLOTS):
            row = label_ref[t, slot, 0].astype(jnp.int32)
            grid_ref[row] += piece_ref[t, 2 * PART * slot : 2 * PART * (slot + 1), :]
    items = [(grid_ref[r, :PART, :], grid_ref[r, PART:, :]) for r in range(TROWS)]
    for x1, (a, b) in enumerate(fft(items)):
        c = twiddle_ref[x1, 0:1, :]
        s = twiddle_ref[x1, 1:2, :]
        rows_ref[x1 * PART : (x1 + 1) * PART, :TILE] = a * c - b * s
        rows_ref[x1 * PART : (x1 + 1) * PART, TILE:] = a * s + b * c
    out = dot3(table_ref[0], table_ref[1], rows_ref[...], NT)
    for half in range(2):
        for part in range(2):
            out_ref[pl.ds(2 * half + part, TILE, stride=4), :] = out[
                part * TILE : (part + 1) * TILE, half * TILE : (half + 1) * TILE
            ]


def transform_v_kernel(data_ref, column_ref, twiddle_ref, table_ref, out_ref, rows_ref):
    items = []
    for g in range(GROUPS):
        u = dot3(column_ref[0, g], column_ref[1, g], data_ref[64 * g : 64 * (g + 1), :], NN)
        items.append((u[:COLUMNS], u[COLUMNS:]))
    for ya, (a, b) in enumerate(fft(items)):
        c = twiddle_ref[ya, 0]
        s = twiddle_ref[ya, 1]
        rows_ref[ya * COLUMNS : (ya + 1) * COLUMNS, :TILE] = a * c - b * s
        rows_ref[ya * COLUMNS : (ya + 1) * COLUMNS, TILE:] = a * s + b * c
    out = dot3(table_ref[0], table_ref[1], rows_ref[...], NT)
    for yb in range(PART):
        for half in range(2):
            out_ref[2 * yb + half] = out[
                yb * 16 : (yb + 1) * 16, half * TILE : (half + 1) * TILE
            ]


def correct_kernel(index_ref, plane_ref, data_ref, real_ref, imaginary_ref):
    rows = real_ref.shape[0]
    x = lax.broadcasted_iota(jnp.int32, (rows, TILE), 0) + index_ref[0] * rows
    y = lax.broadcasted_iota(jnp.int32, (rows, TILE), 1) + index_ref[1] * TILE
    along_l = (x - NU // 2).astype(f32) * (1.0 / NU)
    along_m = (y - NV // 2).astype(f32) * (1.0 / NV)
    height = jnp.sqrt(1.0 - along_l * along_l - along_m * along_m)
    phase = 2.0 * math.pi * plane_ref[0] * (height - 1.0)
    scale = 1.0 / math.sqrt(NU * NV)
    cosine = jnp.cos(phase) * scale
    sine = jnp.sin(phase) * scale
    a = data_ref[:, :8, :].reshape(rows, TILE)
    b = data_ref[:, 8:, :].reshape(rows, TILE)
    real_ref[...] = a * cosine - b * sine
    imaginary_ref[...] = a * sine + b * cosine


VMEM = pl.BlockSpec(memory_space=pltpu.VMEM)
SMEM = pl.BlockSpec(memory_space=pltpu.SMEM)


def call(kernel, outs, in_specs, scratch=(), grid=()):
    single = not isinstance(outs, list)
    return pl.pallas_call(
        kernel,
        out_shape=outs,
        grid=grid,
        in_specs=in_specs,
        out_specs=VMEM if single else [VMEM] * len(outs),
        scratch_shapes=list(scratch),
        compiler_params=pltpu.CompilerParams(vmem_limit_bytes=32 * 1024 * 1024),
    )


def shards(visibilities, coords, tile_row, counts, w_plane):
    def shape(*dims):
        return jax.ShapeDtypeStruct(dims, f32)

    length = 2 * PART * SLOTS + SLOTS
    pieces = call(grid_kernel, shape(GROUPS, length, TILE), [SMEM, SMEM, VMEM, VMEM])(
        counts, tile_row, visibilities, coords
    )
    pieces = lax.all_to_all(pieces, "tm", 0, 0, tiled=True)
    label_spec = pl.BlockSpec(
        (GROUPS, SLOTS, TILE), lambda step: (0, 2 * PART, 0), memory_space=pltpu.SMEM
    )
    spectrum = call(
        transform_u_kernel,
        shape(512, TILE),
        [label_spec, VMEM, VMEM, VMEM],
        [pltpu.VMEM((TROWS + 1, 2 * PART, TILE), f32), pltpu.VMEM((256, 256), f32)],
        (1,),
    )(pieces, pieces, jnp.asarray(inner_u_table()), jnp.asarray(twiddle_u_table()))
    spectrum = lax.all_to_all(
        spectrum.reshape(256, 2, TILE), ("tm", "col"), 0, 0, tiled=True
    ).reshape(512, TILE)
    image = call(
        transform_v_kernel,
        shape(COLUMNS, 16, TILE),
        [VMEM, VMEM, VMEM, VMEM],
        [pltpu.VMEM((256, 256), f32)],
    )(
        spectrum,
        jnp.asarray(column_table()),
        jnp.asarray(twiddle_v_table()),
        jnp.asarray(inner_v_table()),
    )
    image = lax.all_to_all(image, "col", 0, 0, tiled=True)
    index = jnp.stack([lax.axis_index("tm"), lax.axis_index("col")]).astype(jnp.int32)
    rows = NU // GROUPS
    return tuple(
        call(correct_kernel, [shape(rows, TILE)] * 2, [SMEM, SMEM, VMEM])(index, w_plane, image)
    )


def solution(mesh):
    return jax.shard_map(
        shards,
        mesh=mesh,
        in_specs=(
            P("tm", "col", None, None),
            P("tm", "col", None, None),
            P("tm", "col"),
            P("tm", "col"),
            P(),
        ),
        out_specs=(P("tm", "col"), P("tm", "col")),
        check_vma=False,
    )
```

```python
import math

import jax
import jax.numpy as jnp
import numpy as np
from jax import lax
from jax.experimental import pallas as pl
from jax.experimental.pallas import tpu as pltpu
from jax.sharding import PartitionSpec as P

TILE = 128
TROWS = 16
NU = 2048
NV = 4096
GROUPS = 8
COLUMNS = 32
SLOTS = 8
BLOCK = 2048
PART = TILE // GROUPS
CHUNK = 512

f32 = jnp.float32
bf16 = jnp.bfloat16
NT = (((1,), (1,)), ((), ()))
NN = (((1,), (0,)), ((), ()))


def unit(product, length):
    angle = np.mod(product, length) * (2.0 * math.pi / length)
    return np.cos(angle), np.sin(angle)


def split(table):
    table = np.asarray(table, np.float32)
    high = table.astype(jnp.bfloat16)
    low = (table - high.astype(np.float32)).astype(jnp.bfloat16)
    return np.stack([high, low])


def inner_u_table():
    x2 = np.arange(TILE)[:, None]
    i = np.arange(TILE)[None, :]
    c, s = unit(x2 * i, TILE)
    return split(np.block([[c, -s], [s, c]]))


def twiddle_u_table():
    x1 = np.arange(TROWS)[:, None]
    i = np.arange(TILE)[None, :]
    c, s = unit(x1 * i, NU)
    return np.stack([c, s], 1).astype(np.float32)


def column_table():
    y1 = np.arange(COLUMNS)[:, None]
    c = np.arange(COLUMNS)[None, :]
    tables = []
    for g in range(GROUPS):
        co, si = unit(TILE * c * y1 + PART * g * y1, NV)
        t = np.zeros((2, COLUMNS, COLUMNS, 2))
        t[0, :, :, 0], t[0, :, :, 1] = co, -si
        t[1, :, :, 0], t[1, :, :, 1] = si, co
        tables.append(t.reshape(2 * COLUMNS, 2 * COLUMNS))
    return split(np.stack(tables))


def twiddle_v_table():
    ya = np.arange(GROUPS)[:, None, None]
    y1 = np.arange(COLUMNS)[None, :, None]
    j = (np.arange(TILE) % PART)[None, None, :]
    c, s = unit(j * (y1 + COLUMNS * ya), NV)
    return np.stack([c, s], 1).astype(np.float32)


def inner_v_table():
    yb = np.arange(PART)[:, None]
    j = np.arange(PART)[None, :]
    c, s = unit(yb * j, PART)
    t = np.zeros((PART, 2, 8, 2, 8, PART))
    for xx in range(8):
        t[:, 0, xx, 0, xx, :] = c
        t[:, 0, xx, 1, xx, :] = -s
        t[:, 1, xx, 0, xx, :] = s
        t[:, 1, xx, 1, xx, :] = c
    return split(t.reshape(256, 256))


def dot3(a_high, a_low, b, dims):
    b_high = b.astype(bf16)
    b_low = (b - b_high.astype(f32)).astype(bf16)
    def dot(x, y):
        return lax.dot_general(x, y, dims, preferred_element_type=f32)
    return dot(a_high, b_high) + (dot(a_low, b_high) + dot(a_high, b_low))


def fft(items):
    n = len(items)
    if n == 1:
        return items
    even = fft(items[0::2])
    odd = fft(items[1::2])
    out = [None] * n
    for k in range(n // 2):
        er, ei = even[k]
        a, b = odd[k]
        if k == 0:
            tr, ti = a, b
        elif 4 * k == n:
            tr, ti = -b, a
        elif 8 * k == n:
            h = math.sqrt(0.5)
            tr, ti = (a - b) * h, (a + b) * h
        elif 8 * k == 3 * n:
            h = math.sqrt(0.5)
            tr, ti = (a + b) * -h, (a - b) * h
        else:
            c, s = math.cos(2 * math.pi * k / n), math.sin(2 * math.pi * k / n)
            tr, ti = a * c - b * s, a * s + b * c
        out[k] = (er + tr, ei + ti)
        out[k + n // 2] = (er - tr, ei - ti)
    return out


def grid_kernel(
    count_ref, row_hbm, vis_hbm, place_hbm, out_ref, row_ref, vis_ref, place_ref, known, arrived
):
    rows = pltpu.make_async_copy(row_hbm, row_ref, known)
    rows.start()

    def fetch(slot):
        return (
            pltpu.make_async_copy(vis_hbm.at[slot, 0], vis_ref.at[slot], arrived.at[0, slot]),
            pltpu.make_async_copy(place_hbm.at[slot, 0], place_ref.at[slot], arrived.at[1, slot]),
        )

    for slot in range(SLOTS):
        for copy in fetch(slot):
            copy.start()

    def wait(slot, carry):
        for copy in fetch(slot):
            copy.wait()
        return carry

    rows.wait()
    count = count_ref[0, 0]
    slot_of = lax.broadcasted_iota(jnp.int32, (SLOTS, TILE), 0)
    label = jnp.full((SLOTS, TILE), TROWS, jnp.int32)
    for slot in range(SLOTS):
        here = jnp.where(slot < count, row_ref[0, slot], TROWS)
        label = jnp.where(slot_of == slot, here, label)
    label = label.astype(f32)
    for g in range(GROUPS):
        out_ref[g, 2 * PART * SLOTS :, :] = label

    cells = lax.broadcasted_iota(jnp.int32, (TILE, CHUNK), 0).astype(f32)

    def taper(position):
        offset = cells - position
        inside = jnp.maximum(1.0 - offset * offset, 0.0)
        return (inside * inside).astype(bf16)

    def one_slot(slot, carry):
        wait(slot, 0)
        total = jnp.zeros((TILE, 2 * TILE), f32)
        for start in range(0, BLOCK, CHUNK):
            at = pl.ds(start, CHUNK)
            weight_u = taper(place_ref[slot, 0:1, at])
            weight_v = taper(place_ref[slot, 1:2, at])
            real = weight_u * vis_ref[slot, 0:1, at].astype(bf16)
            imaginary = weight_u * vis_ref[slot, 1:2, at].astype(bf16)
            weighted = jnp.concatenate([real, imaginary], 0)
            total += lax.dot_general(weight_v, weighted, NT, preferred_element_type=f32)
        for part in range(2):
            piece = total[:, part * TILE : (part + 1) * TILE].reshape(GROUPS, PART, TILE)
            first = pl.multiple_of(slot * (2 * PART) + part * PART, PART)
            out_ref[:, pl.ds(first, PART), :] = piece
        return carry

    lax.fori_loop(0, count, one_slot, 0)
    lax.fori_loop(count, SLOTS, wait, 0)


def transform_u_kernel(piece_ref, table_ref, twiddle_ref, out_ref, grid_ref, rows_ref):
    grid_ref[...] = jnp.zeros_like(grid_ref)
    for t in range(GROUPS):
        label = piece_ref[t, 2 * PART * SLOTS :, :].astype(jnp.int32)
        for slot in range(SLOTS):
            row = label[slot, 0]
            grid_ref[slot % 2, row] += piece_ref[t, 2 * PART * slot : 2 * PART * (slot + 1), :]
    cells = [grid_ref[0, r] + grid_ref[1, r] for r in range(TROWS)]
    items = [(cell[:PART], cell[PART:]) for cell in cells]
    for x1, (a, b) in enumerate(fft(items)):
        c = twiddle_ref[x1, 0:1, :]
        s = twiddle_ref[x1, 1:2, :]
        rows_ref[x1 * PART : (x1 + 1) * PART, :TILE] = a * c - b * s
        rows_ref[x1 * PART : (x1 + 1) * PART, TILE:] = a * s + b * c
    out = dot3(table_ref[0], table_ref[1], rows_ref[...], NT)
    for half in range(2):
        for part in range(2):
            out_ref[pl.ds(2 * half + part, TILE, stride=4), :] = out[
                part * TILE : (part + 1) * TILE, half * TILE : (half + 1) * TILE
            ]


def transform_v_kernel(data_ref, column_ref, twiddle_ref, table_ref, out_ref, rows_ref):
    items = []
    for g in range(GROUPS):
        u = dot3(column_ref[0, g], column_ref[1, g], data_ref[64 * g : 64 * (g + 1), :], NN)
        items.append((u[:COLUMNS], u[COLUMNS:]))
    for ya, (a, b) in enumerate(fft(items)):
        c = twiddle_ref[ya, 0]
        s = twiddle_ref[ya, 1]
        rows_ref[ya * COLUMNS : (ya + 1) * COLUMNS, :TILE] = a * c - b * s
        rows_ref[ya * COLUMNS : (ya + 1) * COLUMNS, TILE:] = a * s + b * c
    out = dot3(table_ref[0], table_ref[1], rows_ref[...], NT)
    for yb in range(PART):
        for half in range(2):
            out_ref[2 * yb + half] = out[
                yb * 16 : (yb + 1) * 16, half * TILE : (half + 1) * TILE
            ]


def phase_factors(plane, x, y):
    along_l = (x - NU // 2).astype(f32) / NU
    along_m = (y - NV // 2).astype(f32) / NV
    height = jnp.sqrt(
        1.0 - along_l[:, None] * along_l[:, None] - along_m[None, :] * along_m[None, :]
    )
    phase = 2.0 * math.pi * plane * (height - 1.0)
    scale = 1.0 / math.sqrt(NU * NV)
    return lax.optimization_barrier((jnp.cos(phase) * scale, jnp.sin(phase) * scale))


VMEM = pl.BlockSpec(memory_space=pltpu.VMEM)
SMEM = pl.BlockSpec(memory_space=pltpu.SMEM)
HBM = pl.BlockSpec(memory_space=pltpu.HBM)


def call(kernel, outs, in_specs, scratch=(), vmem=32):
    return pl.pallas_call(
        kernel,
        out_shape=outs,
        in_specs=in_specs,
        out_specs=VMEM,
        scratch_shapes=list(scratch),
        compiler_params=pltpu.CompilerParams(vmem_limit_bytes=vmem * 1024 * 1024),
    )


def shards(visibilities, coords, tile_row, counts, w_plane):
    def shape(*dims):
        return jax.ShapeDtypeStruct(dims, f32)

    length = 2 * PART * SLOTS + SLOTS
    pieces = call(
        grid_kernel,
        shape(GROUPS, length, TILE),
        [SMEM, HBM, HBM, HBM],
        [
            pltpu.SMEM((1, SLOTS), jnp.int32),
            pltpu.VMEM((SLOTS, 2, BLOCK), f32),
            pltpu.VMEM((SLOTS, 2, BLOCK), f32),
            pltpu.SemaphoreType.DMA(()),
            pltpu.SemaphoreType.DMA((2, SLOTS)),
        ],
    )(
        counts,
        pltpu.with_memory_space_constraint(tile_row.reshape(1, SLOTS), pltpu.HBM),
        pltpu.with_memory_space_constraint(visibilities, pltpu.HBM),
        pltpu.with_memory_space_constraint(coords, pltpu.HBM),
    )
    pieces = lax.all_to_all(pieces, "tm", 0, 0, tiled=True)
    spectrum = call(
        transform_u_kernel,
        shape(512, TILE),
        [VMEM, VMEM, VMEM],
        [pltpu.VMEM((2, TROWS + 1, 2 * PART, TILE), f32), pltpu.VMEM((256, 256), f32)],
    )(pieces, jnp.asarray(inner_u_table()), jnp.asarray(twiddle_u_table()))
    spectrum = lax.all_to_all(
        spectrum.reshape(256, 2, TILE), ("tm", "col"), 0, 0, tiled=True
    ).reshape(512, TILE)
    image = call(
        transform_v_kernel,
        shape(COLUMNS, 16, TILE),
        [VMEM, VMEM, VMEM, VMEM],
        [pltpu.VMEM((256, 256), f32)],
    )(
        spectrum,
        jnp.asarray(column_table()),
        jnp.asarray(twiddle_v_table()),
        jnp.asarray(inner_v_table()),
    )
    image = lax.all_to_all(image, "col", 0, 0, tiled=True)
    rows = NU // GROUPS
    x = lax.axis_index("tm") * rows + jnp.arange(rows, dtype=jnp.int32)
    y = lax.axis_index("col") * TILE + jnp.arange(TILE, dtype=jnp.int32)
    cosine, sine = phase_factors(w_plane[0], x, y)
    real = image[:, :8, :].reshape(rows, TILE)
    imaginary = image[:, 8:, :].reshape(rows, TILE)
    return real * cosine - imaginary * sine, real * sine + imaginary * cosine


def solution(mesh):
    return jax.shard_map(
        shards,
        mesh=mesh,
        in_specs=(
            P("tm", "col", None, None),
            P("tm", "col", None, None),
            P("tm", "col"),
            P("tm", "col"),
            P(),
        ),
        out_specs=(P("tm", "col"), P("tm", "col")),
        check_vma=False,
    )
```

```python
import math

import jax
import jax.numpy as jnp
import numpy as np
from jax import lax
from jax.experimental import pallas as pl
from jax.experimental.pallas import tpu as pltpu
from jax.sharding import PartitionSpec as P

TILE = 128
TROWS = 16
NU = 2048
NV = 4096
GROUPS = 8
COLUMNS = 32
SLOTS = 8
BLOCK = 2048
PART = TILE // GROUPS
CHUNK = 512

f32 = jnp.float32
bf16 = jnp.bfloat16
NT = (((1,), (1,)), ((), ()))
NN = (((1,), (0,)), ((), ()))


def unit(product, length):
    angle = np.mod(product, length) * (2.0 * math.pi / length)
    return np.cos(angle), np.sin(angle)


def split(table):
    table = np.asarray(table, np.float32)
    high = table.astype(jnp.bfloat16)
    low = (table - high.astype(np.float32)).astype(jnp.bfloat16)
    return np.stack([high, low])


def inner_u_table():
    x2 = np.arange(TILE)[:, None]
    i = np.arange(TILE)[None, :]
    c, s = unit(x2 * i, TILE)
    return split(np.block([[c, -s], [s, c]]))


def twiddle_u_table():
    x1 = np.arange(TROWS)[:, None]
    i = np.arange(TILE)[None, :]
    c, s = unit(x1 * i, NU)
    return np.stack([c, s], 1).astype(np.float32)


def column_table():
    y1 = np.arange(COLUMNS)[:, None]
    c = np.arange(COLUMNS)[None, :]
    tables = []
    for g in range(GROUPS):
        co, si = unit(TILE * c * y1 + PART * g * y1, NV)
        t = np.zeros((2, COLUMNS, COLUMNS, 2))
        t[0, :, :, 0], t[0, :, :, 1] = co, -si
        t[1, :, :, 0], t[1, :, :, 1] = si, co
        tables.append(t.reshape(2 * COLUMNS, 2 * COLUMNS))
    return split(np.stack(tables))


def twiddle_v_table():
    ya = np.arange(GROUPS)[:, None, None]
    y1 = np.arange(COLUMNS)[None, :, None]
    j = (np.arange(TILE) % PART)[None, None, :]
    c, s = unit(j * (y1 + COLUMNS * ya), NV)
    return np.stack([c, s], 1).astype(np.float32)


def inner_v_table():
    yb = np.arange(PART)[:, None]
    j = np.arange(PART)[None, :]
    c, s = unit(yb * j, PART)
    t = np.zeros((PART, 2, 8, 2, 8, PART))
    for xx in range(8):
        t[:, 0, xx, 0, xx, :] = c
        t[:, 0, xx, 1, xx, :] = -s
        t[:, 1, xx, 0, xx, :] = s
        t[:, 1, xx, 1, xx, :] = c
    return split(t.reshape(256, 256))


def dot3(a_high, a_low, b, dims):
    b_high = b.astype(bf16)
    b_low = (b - b_high.astype(f32)).astype(bf16)
    def dot(x, y):
        return lax.dot_general(x, y, dims, preferred_element_type=f32)
    return dot(a_high, b_high) + (dot(a_low, b_high) + dot(a_high, b_low))


def fft(items):
    n = len(items)
    if n == 1:
        return items
    even = fft(items[0::2])
    odd = fft(items[1::2])
    out = [None] * n
    for k in range(n // 2):
        er, ei = even[k]
        a, b = odd[k]
        if k == 0:
            tr, ti = a, b
        elif 4 * k == n:
            tr, ti = -b, a
        elif 8 * k == n:
            h = math.sqrt(0.5)
            tr, ti = (a - b) * h, (a + b) * h
        elif 8 * k == 3 * n:
            h = math.sqrt(0.5)
            tr, ti = (a + b) * -h, (a - b) * h
        else:
            c, s = math.cos(2 * math.pi * k / n), math.sin(2 * math.pi * k / n)
            tr, ti = a * c - b * s, a * s + b * c
        out[k] = (er + tr, ei + ti)
        out[k + n // 2] = (er - tr, ei - ti)
    return out


def grid_kernel(
    count_ref, row_hbm, vis_hbm, place_hbm, out_ref, row_ref, vis_ref, place_ref, known, arrived
):
    rows = pltpu.make_async_copy(row_hbm, row_ref, known)
    rows.start()

    def fetch(slot):
        return (
            pltpu.make_async_copy(vis_hbm.at[slot, 0], vis_ref.at[slot], arrived.at[0, slot]),
            pltpu.make_async_copy(place_hbm.at[slot, 0], place_ref.at[slot], arrived.at[1, slot]),
        )

    for slot in range(SLOTS):
        for copy in fetch(slot):
            copy.start()

    def wait(slot, carry):
        for copy in fetch(slot):
            copy.wait()
        return carry

    rows.wait()
    count = count_ref[0, 0]
    for slot in range(SLOTS):
        row = jnp.where(slot < count, row_ref[0, slot], TROWS).astype(f32)
        out_ref[:, 2 * PART * slot : 2 * PART * slot + 8, :] = jnp.full((GROUPS, 8, TILE), row)

    cells = lax.broadcasted_iota(jnp.int32, (TILE, CHUNK), 0).astype(f32)

    def taper(position):
        offset = cells - position
        inside = jnp.maximum(1.0 - offset * offset, 0.0)
        return (inside * inside).astype(bf16)

    corner = lax.broadcasted_iota(jnp.int32, (GROUPS, PART, TILE), 2) == 0

    def one_slot(slot, carry):
        wait(slot, 0)
        total = jnp.zeros((TILE, 2 * TILE), f32)
        for start in range(0, BLOCK, CHUNK):
            at = pl.ds(start, CHUNK)
            weight_u = taper(place_ref[slot, 0:1, at])
            weight_v = taper(place_ref[slot, 1:2, at])
            real = weight_u * vis_ref[slot, 0:1, at].astype(bf16)
            imaginary = weight_u * vis_ref[slot, 1:2, at].astype(bf16)
            weighted = jnp.concatenate([real, imaginary], 0)
            total += lax.dot_general(weight_v, weighted, NT, preferred_element_type=f32)
        for part in range(2):
            piece = total[:, part * TILE : (part + 1) * TILE].reshape(GROUPS, PART, TILE)
            if part == 0:
                piece = jnp.where(corner, row_ref[0, slot].astype(f32), piece)
            first = pl.multiple_of(slot * (2 * PART) + part * PART, PART)
            out_ref[:, pl.ds(first, PART), :] = piece
        return carry

    lax.fori_loop(0, count, one_slot, 0)
    lax.fori_loop(count, SLOTS, wait, 0)


def transform_u_kernel(piece_ref, table_ref, twiddle_ref, out_ref, grid_ref, rows_ref):
    grid_ref[...] = jnp.zeros_like(grid_ref)
    for t in range(GROUPS):
        for slot in range(SLOTS):
            piece = piece_ref[t, 2 * PART * slot : 2 * PART * (slot + 1), :]
            row = piece[0, 0].astype(jnp.int32)
            grid_ref[slot % 2, row] += piece
    cells = [grid_ref[0, r] + grid_ref[1, r] for r in range(TROWS)]
    reached = lax.broadcasted_iota(jnp.int32, (PART, TILE), 1) > 0
    items = [(jnp.where(reached, cell[:PART], 0.0), cell[PART:]) for cell in cells]
    for x1, (a, b) in enumerate(fft(items)):
        c = twiddle_ref[x1, 0:1, :]
        s = twiddle_ref[x1, 1:2, :]
        rows_ref[x1 * PART : (x1 + 1) * PART, :TILE] = a * c - b * s
        rows_ref[x1 * PART : (x1 + 1) * PART, TILE:] = a * s + b * c
    out = dot3(table_ref[0], table_ref[1], rows_ref[...], NT)
    for half in range(2):
        for part in range(2):
            out_ref[pl.ds(2 * half + part, TILE, stride=4), :] = out[
                part * TILE : (part + 1) * TILE, half * TILE : (half + 1) * TILE
            ]


def transform_v_kernel(data_ref, column_ref, twiddle_ref, table_ref, out_ref, rows_ref):
    items = []
    for g in range(GROUPS):
        u = dot3(column_ref[0, g], column_ref[1, g], data_ref[64 * g : 64 * (g + 1), :], NN)
        items.append((u[:COLUMNS], u[COLUMNS:]))
    for ya, (a, b) in enumerate(fft(items)):
        c = twiddle_ref[ya, 0]
        s = twiddle_ref[ya, 1]
        rows_ref[ya * COLUMNS : (ya + 1) * COLUMNS, :TILE] = a * c - b * s
        rows_ref[ya * COLUMNS : (ya + 1) * COLUMNS, TILE:] = a * s + b * c
    out = dot3(table_ref[0], table_ref[1], rows_ref[...], NT)
    for yb in range(PART):
        for half in range(2):
            out_ref[2 * yb + half] = out[
                yb * 16 : (yb + 1) * 16, half * TILE : (half + 1) * TILE
            ]


def phase_factors(plane, x, y):
    along_l = (x - NU // 2).astype(f32) / NU
    along_m = (y - NV // 2).astype(f32) / NV
    height = jnp.sqrt(
        1.0 - along_l[:, None] * along_l[:, None] - along_m[None, :] * along_m[None, :]
    )
    phase = 2.0 * math.pi * plane * (height - 1.0)
    scale = 1.0 / math.sqrt(NU * NV)
    return lax.optimization_barrier((jnp.cos(phase) * scale, jnp.sin(phase) * scale))


VMEM = pl.BlockSpec(memory_space=pltpu.VMEM)
SMEM = pl.BlockSpec(memory_space=pltpu.SMEM)
HBM = pl.BlockSpec(memory_space=pltpu.HBM)


def call(kernel, outs, in_specs, scratch=(), vmem=32):
    return pl.pallas_call(
        kernel,
        out_shape=outs,
        in_specs=in_specs,
        out_specs=VMEM,
        scratch_shapes=list(scratch),
        compiler_params=pltpu.CompilerParams(vmem_limit_bytes=vmem * 1024 * 1024),
    )


def shards(visibilities, coords, tile_row, counts, w_plane):
    def shape(*dims):
        return jax.ShapeDtypeStruct(dims, f32)

    length = 2 * PART * SLOTS
    pieces = call(
        grid_kernel,
        shape(GROUPS, length, TILE),
        [SMEM, HBM, HBM, HBM],
        [
            pltpu.SMEM((1, SLOTS), jnp.int32),
            pltpu.VMEM((SLOTS, 2, BLOCK), f32),
            pltpu.VMEM((SLOTS, 2, BLOCK), f32),
            pltpu.SemaphoreType.DMA(()),
            pltpu.SemaphoreType.DMA((2, SLOTS)),
        ],
    )(
        counts,
        pltpu.with_memory_space_constraint(tile_row.reshape(1, SLOTS), pltpu.HBM),
        pltpu.with_memory_space_constraint(visibilities, pltpu.HBM),
        pltpu.with_memory_space_constraint(coords, pltpu.HBM),
    )
    pieces = lax.all_to_all(pieces, "tm", 0, 0, tiled=True)
    spectrum = call(
        transform_u_kernel,
        shape(512, TILE),
        [VMEM, VMEM, VMEM],
        [pltpu.VMEM((2, TROWS + 1, 2 * PART, TILE), f32), pltpu.VMEM((256, 256), f32)],
    )(pieces, jnp.asarray(inner_u_table()), jnp.asarray(twiddle_u_table()))
    spectrum = lax.all_to_all(
        spectrum.reshape(256, 2, TILE), ("tm", "col"), 0, 0, tiled=True
    ).reshape(512, TILE)
    image = call(
        transform_v_kernel,
        shape(COLUMNS, 16, TILE),
        [VMEM, VMEM, VMEM, VMEM],
        [pltpu.VMEM((256, 256), f32)],
    )(
        spectrum,
        jnp.asarray(column_table()),
        jnp.asarray(twiddle_v_table()),
        jnp.asarray(inner_v_table()),
    )
    image = lax.all_to_all(image, "col", 0, 0, tiled=True)
    rows = NU // GROUPS
    x = lax.axis_index("tm") * rows + jnp.arange(rows, dtype=jnp.int32)
    y = lax.axis_index("col") * TILE + jnp.arange(TILE, dtype=jnp.int32)
    cosine, sine = phase_factors(w_plane[0], x, y)
    real = image[:, :8, :].reshape(rows, TILE)
    imaginary = image[:, 8:, :].reshape(rows, TILE)
    return real * cosine - imaginary * sine, real * sine + imaginary * cosine


def solution(mesh):
    return jax.shard_map(
        shards,
        mesh=mesh,
        in_specs=(
            P("tm", "col", None, None),
            P("tm", "col", None, None),
            P("tm", "col"),
            P("tm", "col"),
            P(),
        ),
        out_specs=(P("tm", "col"), P("tm", "col")),
        check_vma=False,
    )
```

```python
import math

import jax
import jax.numpy as jnp
import numpy as np
from jax import lax
from jax.experimental import pallas as pl
from jax.experimental.pallas import tpu as pltpu
from jax.sharding import PartitionSpec as P

TILE = 128
TROWS = 16
NU = 2048
NV = 4096
GROUPS = 8
COLUMNS = 32
SLOTS = 8
BLOCK = 2048
PART = TILE // GROUPS
CHUNK = 512

f32 = jnp.float32
bf16 = jnp.bfloat16
NT = (((1,), (1,)), ((), ()))
NN = (((1,), (0,)), ((), ()))


def unit(product, length):
    angle = np.mod(product, length) * (2.0 * math.pi / length)
    return np.cos(angle), np.sin(angle)


def split(table):
    table = np.asarray(table, np.float32)
    high = table.astype(jnp.bfloat16)
    low = (table - high.astype(np.float32)).astype(jnp.bfloat16)
    return np.stack([high, low])


def inner_u_table():
    x2 = np.arange(TILE)[:, None]
    i = np.arange(TILE)[None, :]
    c, s = unit(x2 * i, TILE)
    return split(np.block([[c, -s], [s, c]]))


def twiddle_u_table():
    x1 = np.arange(TROWS)[:, None]
    i = np.arange(TILE)[None, :]
    c, s = unit(x1 * i, NU)
    return np.stack([c, s], 1).astype(np.float32)


def column_table():
    y1 = np.arange(COLUMNS)[:, None]
    c = np.arange(COLUMNS)[None, :]
    tables = []
    for g in range(GROUPS):
        co, si = unit(TILE * c * y1 + PART * g * y1, NV)
        t = np.zeros((2, COLUMNS, COLUMNS, 2))
        t[0, :, :, 0], t[0, :, :, 1] = co, -si
        t[1, :, :, 0], t[1, :, :, 1] = si, co
        tables.append(t.reshape(2 * COLUMNS, 2 * COLUMNS))
    return split(np.stack(tables))


def twiddle_v_table():
    ya = np.arange(GROUPS)[:, None, None]
    y1 = np.arange(COLUMNS)[None, :, None]
    j = (np.arange(TILE) % PART)[None, None, :]
    c, s = unit(j * (y1 + COLUMNS * ya), NV)
    return np.stack([c, s], 1).astype(np.float32)


def inner_v_table():
    yb = np.arange(PART)[:, None]
    j = np.arange(PART)[None, :]
    c, s = unit(yb * j, PART)
    t = np.zeros((PART, 2, 8, 2, 8, PART))
    for xx in range(8):
        t[:, 0, xx, 0, xx, :] = c
        t[:, 0, xx, 1, xx, :] = -s
        t[:, 1, xx, 0, xx, :] = s
        t[:, 1, xx, 1, xx, :] = c
    return split(t.reshape(256, 256))


def dot3(a_high, a_low, b, dims):
    b_high = b.astype(bf16)
    b_low = (b - b_high.astype(f32)).astype(bf16)
    def dot(x, y):
        return lax.dot_general(x, y, dims, preferred_element_type=f32)
    return dot(a_high, b_high) + (dot(a_low, b_high) + dot(a_high, b_low))


def fft(items):
    n = len(items)
    if n == 1:
        return items
    even = fft(items[0::2])
    odd = fft(items[1::2])
    out = [None] * n
    for k in range(n // 2):
        er, ei = even[k]
        a, b = odd[k]
        if k == 0:
            tr, ti = a, b
        elif 4 * k == n:
            tr, ti = -b, a
        elif 8 * k == n:
            h = math.sqrt(0.5)
            tr, ti = (a - b) * h, (a + b) * h
        elif 8 * k == 3 * n:
            h = math.sqrt(0.5)
            tr, ti = (a + b) * -h, (a - b) * h
        else:
            c, s = math.cos(2 * math.pi * k / n), math.sin(2 * math.pi * k / n)
            tr, ti = a * c - b * s, a * s + b * c
        out[k] = (er + tr, ei + ti)
        out[k + n // 2] = (er - tr, ei - ti)
    return out


def grid_kernel(
    count_ref, row_hbm, vis_hbm, place_hbm, out_ref, row_ref, vis_ref, place_ref, known, arrived
):
    rows = pltpu.make_async_copy(row_hbm, row_ref, known)
    rows.start()

    def fetch(slot):
        return (
            pltpu.make_async_copy(vis_hbm.at[slot, 0], vis_ref.at[slot], arrived.at[0, slot]),
            pltpu.make_async_copy(place_hbm.at[slot, 0], place_ref.at[slot], arrived.at[1, slot]),
        )

    for slot in range(SLOTS):
        for copy in fetch(slot):
            copy.start()

    def wait(slot, carry):
        for copy in fetch(slot):
            copy.wait()
        return carry

    rows.wait()
    count = count_ref[0, 0]
    for slot in range(SLOTS):
        row = jnp.where(slot < count, row_ref[0, slot], TROWS).astype(f32)
        out_ref[:, 2 * PART * slot : 2 * PART * slot + 8, :] = jnp.full((GROUPS, 8, TILE), row)

    cells = lax.broadcasted_iota(jnp.int32, (TILE, CHUNK), 0).astype(f32).astype(bf16)
    none = jnp.zeros((TILE, CHUNK), bf16)

    def taper(offset):
        inside = jnp.maximum(1.0 - offset * offset, 0.0)
        return (inside * inside).astype(bf16)

    def reached(position):
        first = jnp.floor(position)
        second = first + 1.0
        return (
            (cells == first.astype(bf16), taper(first - position)),
            (cells == second.astype(bf16), taper(second - position)),
        )

    def spread(places, values):
        return jnp.where(places[0], values[0], jnp.where(places[1], values[1], none))

    corner = lax.broadcasted_iota(jnp.int32, (GROUPS, PART, TILE), 2) == 0

    def one_slot(slot, carry):
        wait(slot, 0)
        total = jnp.zeros((TILE, 2 * TILE), f32)
        for start in range(0, BLOCK, CHUNK):
            at = pl.ds(start, CHUNK)
            (here_u, first_u), (next_u, second_u) = reached(place_ref[slot, 0:1, at])
            (here_v, first_v), (next_v, second_v) = reached(place_ref[slot, 1:2, at])
            weight_v = spread((here_v, next_v), (first_v, second_v))
            first_u, second_u = first_u.astype(f32), second_u.astype(f32)
            real, imaginary = (
                spread(
                    (here_u, next_u),
                    ((first_u * value).astype(bf16), (second_u * value).astype(bf16)),
                )
                for value in (vis_ref[slot, 0:1, at], vis_ref[slot, 1:2, at])
            )
            weighted = jnp.concatenate([real, imaginary], 0)
            total += lax.dot_general(weight_v, weighted, NT, preferred_element_type=f32)
        for part in range(2):
            piece = total[:, part * TILE : (part + 1) * TILE].reshape(GROUPS, PART, TILE)
            if part == 0:
                piece = jnp.where(corner, row_ref[0, slot].astype(f32), piece)
            first = pl.multiple_of(slot * (2 * PART) + part * PART, PART)
            out_ref[:, pl.ds(first, PART), :] = piece
        return carry

    lax.fori_loop(0, count, one_slot, 0)
    lax.fori_loop(count, SLOTS, wait, 0)


def transform_u_kernel(piece_ref, table_ref, twiddle_ref, out_ref, grid_ref, rows_ref):
    grid_ref[...] = jnp.zeros_like(grid_ref)
    for t in range(GROUPS):
        for slot in range(SLOTS):
            piece = piece_ref[t, 2 * PART * slot : 2 * PART * (slot + 1), :]
            row = piece[0, 0].astype(jnp.int32)
            grid_ref[slot % 2, row] += piece
    cells = [grid_ref[0, r] + grid_ref[1, r] for r in range(TROWS)]
    reached = lax.broadcasted_iota(jnp.int32, (PART, TILE), 1) > 0
    items = [(jnp.where(reached, cell[:PART], 0.0), cell[PART:]) for cell in cells]
    for x1, (a, b) in enumerate(fft(items)):
        c = twiddle_ref[x1, 0:1, :]
        s = twiddle_ref[x1, 1:2, :]
        rows_ref[x1 * PART : (x1 + 1) * PART, :TILE] = a * c - b * s
        rows_ref[x1 * PART : (x1 + 1) * PART, TILE:] = a * s + b * c
    out = dot3(table_ref[0], table_ref[1], rows_ref[...], NT)
    for half in range(2):
        for part in range(2):
            out_ref[pl.ds(2 * half + part, TILE, stride=4), :] = out[
                part * TILE : (part + 1) * TILE, half * TILE : (half + 1) * TILE
            ]


def transform_v_kernel(data_ref, column_ref, twiddle_ref, table_ref, out_ref, rows_ref):
    items = []
    for g in range(GROUPS):
        u = dot3(column_ref[0, g], column_ref[1, g], data_ref[64 * g : 64 * (g + 1), :], NN)
        items.append((u[:COLUMNS], u[COLUMNS:]))
    for ya, (a, b) in enumerate(fft(items)):
        c = twiddle_ref[ya, 0]
        s = twiddle_ref[ya, 1]
        rows_ref[ya * COLUMNS : (ya + 1) * COLUMNS, :TILE] = a * c - b * s
        rows_ref[ya * COLUMNS : (ya + 1) * COLUMNS, TILE:] = a * s + b * c
    out = dot3(table_ref[0], table_ref[1], rows_ref[...], NT)
    for yb in range(PART):
        for half in range(2):
            out_ref[2 * yb + half] = out[
                yb * 16 : (yb + 1) * 16, half * TILE : (half + 1) * TILE
            ]


def phase_factors(plane, x, y):
    along_l = (x - NU // 2).astype(f32) / NU
    along_m = (y - NV // 2).astype(f32) / NV
    height = jnp.sqrt(
        1.0 - along_l[:, None] * along_l[:, None] - along_m[None, :] * along_m[None, :]
    )
    phase = 2.0 * math.pi * plane * (height - 1.0)
    scale = 1.0 / math.sqrt(NU * NV)
    return lax.optimization_barrier((jnp.cos(phase) * scale, jnp.sin(phase) * scale))


VMEM = pl.BlockSpec(memory_space=pltpu.VMEM)
SMEM = pl.BlockSpec(memory_space=pltpu.SMEM)
HBM = pl.BlockSpec(memory_space=pltpu.HBM)


def call(kernel, outs, in_specs, scratch=(), vmem=32):
    return pl.pallas_call(
        kernel,
        out_shape=outs,
        in_specs=in_specs,
        out_specs=VMEM,
        scratch_shapes=list(scratch),
        compiler_params=pltpu.CompilerParams(vmem_limit_bytes=vmem * 1024 * 1024),
    )


def shards(visibilities, coords, tile_row, counts, w_plane):
    def shape(*dims):
        return jax.ShapeDtypeStruct(dims, f32)

    length = 2 * PART * SLOTS
    pieces = call(
        grid_kernel,
        shape(GROUPS, length, TILE),
        [SMEM, HBM, HBM, HBM],
        [
            pltpu.SMEM((1, SLOTS), jnp.int32),
            pltpu.VMEM((SLOTS, 2, BLOCK), f32),
            pltpu.VMEM((SLOTS, 2, BLOCK), f32),
            pltpu.SemaphoreType.DMA(()),
            pltpu.SemaphoreType.DMA((2, SLOTS)),
        ],
    )(
        counts,
        pltpu.with_memory_space_constraint(tile_row.reshape(1, SLOTS), pltpu.HBM),
        pltpu.with_memory_space_constraint(visibilities, pltpu.HBM),
        pltpu.with_memory_space_constraint(coords, pltpu.HBM),
    )
    pieces = lax.all_to_all(pieces, "tm", 0, 0, tiled=True)
    spectrum = call(
        transform_u_kernel,
        shape(512, TILE),
        [VMEM, VMEM, VMEM],
        [pltpu.VMEM((2, TROWS + 1, 2 * PART, TILE), f32), pltpu.VMEM((256, 256), f32)],
    )(pieces, jnp.asarray(inner_u_table()), jnp.asarray(twiddle_u_table()))
    spectrum = lax.all_to_all(
        spectrum.reshape(256, 2, TILE), ("tm", "col"), 0, 0, tiled=True
    ).reshape(512, TILE)
    image = call(
        transform_v_kernel,
        shape(COLUMNS, 16, TILE),
        [VMEM, VMEM, VMEM, VMEM],
        [pltpu.VMEM((256, 256), f32)],
    )(
        spectrum,
        jnp.asarray(column_table()),
        jnp.asarray(twiddle_v_table()),
        jnp.asarray(inner_v_table()),
    )
    image = lax.all_to_all(image, "col", 0, 0, tiled=True)
    rows = NU // GROUPS
    x = lax.axis_index("tm") * rows + jnp.arange(rows, dtype=jnp.int32)
    y = lax.axis_index("col") * TILE + jnp.arange(TILE, dtype=jnp.int32)
    cosine, sine = phase_factors(w_plane[0], x, y)
    real = image[:, :8, :].reshape(rows, TILE)
    imaginary = image[:, 8:, :].reshape(rows, TILE)
    return real * cosine - imaginary * sine, real * sine + imaginary * cosine


def solution(mesh):
    return jax.shard_map(
        shards,
        mesh=mesh,
        in_specs=(
            P("tm", "col", None, None),
            P("tm", "col", None, None),
            P("tm", "col"),
            P("tm", "col"),
            P(),
        ),
        out_specs=(P("tm", "col"), P("tm", "col")),
        check_vma=False,
    )
```

```python
import math

import jax
import jax.numpy as jnp
import numpy as np
from jax import lax
from jax.experimental import pallas as pl
from jax.experimental.pallas import tpu as pltpu
from jax.sharding import PartitionSpec as P

TILE = 128
TROWS = 16
NU = 2048
NV = 4096
GROUPS = 8
COLUMNS = 32
SLOTS = 8
BLOCK = 2048
PART = TILE // GROUPS
CHUNK = 512

f32 = jnp.float32
bf16 = jnp.bfloat16
NT = (((1,), (1,)), ((), ()))
NN = (((1,), (0,)), ((), ()))


def unit(product, length):
    angle = np.mod(product, length) * (2.0 * math.pi / length)
    return np.cos(angle), np.sin(angle)


def split(table):
    table = np.asarray(table, np.float32)
    high = table.astype(jnp.bfloat16)
    low = (table - high.astype(np.float32)).astype(jnp.bfloat16)
    return np.stack([high, low])


def inner_u_table():
    x2 = np.arange(TILE)[:, None]
    i = np.arange(TILE)[None, :]
    c, s = unit(x2 * i, TILE)
    return split(np.block([[c, -s], [s, c]]))


def twiddle_u_table():
    x1 = np.arange(TROWS)[:, None]
    i = np.arange(TILE)[None, :]
    c, s = unit(x1 * i, NU)
    return np.stack([c, s], 1).astype(np.float32)


def column_table():
    y1 = np.arange(COLUMNS)[:, None]
    c = np.arange(COLUMNS)[None, :]
    tables = []
    for g in range(GROUPS):
        co, si = unit(TILE * c * y1 + PART * g * y1, NV)
        t = np.zeros((2, COLUMNS, COLUMNS, 2))
        t[0, :, :, 0], t[0, :, :, 1] = co, -si
        t[1, :, :, 0], t[1, :, :, 1] = si, co
        tables.append(t.reshape(2 * COLUMNS, 2 * COLUMNS))
    return split(np.stack(tables))


def twiddle_v_table():
    ya = np.arange(GROUPS)[:, None, None]
    y1 = np.arange(COLUMNS)[None, :, None]
    j = (np.arange(TILE) % PART)[None, None, :]
    c, s = unit(j * (y1 + COLUMNS * ya), NV)
    return np.stack([c, s], 1).astype(np.float32)


def inner_v_table():
    yb = np.arange(PART)[:, None]
    j = np.arange(PART)[None, :]
    c, s = unit(yb * j, PART)
    t = np.zeros((PART, 2, 8, 2, 8, PART))
    for xx in range(8):
        t[:, 0, xx, 0, xx, :] = c
        t[:, 0, xx, 1, xx, :] = -s
        t[:, 1, xx, 0, xx, :] = s
        t[:, 1, xx, 1, xx, :] = c
    return split(t.reshape(256, 256))


def dot3(a_high, a_low, b, dims):
    b_high = b.astype(bf16)
    b_low = (b - b_high.astype(f32)).astype(bf16)
    def dot(x, y):
        return lax.dot_general(x, y, dims, preferred_element_type=f32)
    return dot(a_high, b_high) + (dot(a_low, b_high) + dot(a_high, b_low))


def fft(items):
    n = len(items)
    if n == 1:
        return items
    even = fft(items[0::2])
    odd = fft(items[1::2])
    out = [None] * n
    for k in range(n // 2):
        er, ei = even[k]
        a, b = odd[k]
        if k == 0:
            tr, ti = a, b
        elif 4 * k == n:
            tr, ti = -b, a
        elif 8 * k == n:
            h = math.sqrt(0.5)
            tr, ti = (a - b) * h, (a + b) * h
        elif 8 * k == 3 * n:
            h = math.sqrt(0.5)
            tr, ti = (a + b) * -h, (a - b) * h
        else:
            c, s = math.cos(2 * math.pi * k / n), math.sin(2 * math.pi * k / n)
            tr, ti = a * c - b * s, a * s + b * c
        out[k] = (er + tr, ei + ti)
        out[k + n // 2] = (er - tr, ei - ti)
    return out


def grid_kernel(
    count_ref, row_hbm, vis_hbm, place_hbm, out_ref, row_ref, vis_ref, place_ref, known, arrived
):
    rows = pltpu.make_async_copy(row_hbm, row_ref, known)
    rows.start()

    fetches = (
        pltpu.make_async_copy(place_hbm, place_ref, arrived.at[0]),
        pltpu.make_async_copy(vis_hbm, vis_ref, arrived.at[1]),
    )
    for copy in fetches:
        copy.start()

    rows.wait()
    count = count_ref[0, 0]
    for slot in range(SLOTS):
        row = jnp.where(slot < count, row_ref[0, slot], TROWS).astype(f32)
        out_ref[:, 2 * PART * slot : 2 * PART * slot + 8, :] = jnp.full((GROUPS, 8, TILE), row)

    cells = lax.broadcasted_iota(jnp.int32, (TILE, CHUNK), 0).astype(f32).astype(bf16)
    none = jnp.zeros((TILE, CHUNK), bf16)

    def taper(offset):
        inside = jnp.maximum(1.0 - offset * offset, 0.0)
        return (inside * inside).astype(bf16)

    def reached(position):
        first = jnp.floor(position)
        second = first + 1.0
        return (
            (cells == first.astype(bf16), taper(first - position)),
            (cells == second.astype(bf16), taper(second - position)),
        )

    def spread(places, values):
        return jnp.where(places[0], values[0], jnp.where(places[1], values[1], none))

    corner = lax.broadcasted_iota(jnp.int32, (GROUPS, PART, TILE), 2) == 0

    def one_slot(slot, carry):
        total = jnp.zeros((TILE, 2 * TILE), f32)
        for start in range(0, BLOCK, CHUNK):
            at = pl.ds(start, CHUNK)
            (here_u, first_u), (next_u, second_u) = reached(place_ref[slot, 0, 0:1, at])
            (here_v, first_v), (next_v, second_v) = reached(place_ref[slot, 0, 1:2, at])
            weight_v = spread((here_v, next_v), (first_v, second_v))
            first_u, second_u = first_u.astype(f32), second_u.astype(f32)
            real, imaginary = (
                spread(
                    (here_u, next_u),
                    ((first_u * value).astype(bf16), (second_u * value).astype(bf16)),
                )
                for value in (vis_ref[slot, 0, 0:1, at], vis_ref[slot, 0, 1:2, at])
            )
            weighted = jnp.concatenate([real, imaginary], 0)
            total += lax.dot_general(weight_v, weighted, NT, preferred_element_type=f32)
        for part in range(2):
            piece = total[:, part * TILE : (part + 1) * TILE].reshape(GROUPS, PART, TILE)
            if part == 0:
                piece = jnp.where(corner, row_ref[0, slot].astype(f32), piece)
            first = pl.multiple_of(slot * (2 * PART) + part * PART, PART)
            out_ref[:, pl.ds(first, PART), :] = piece
        return carry

    for copy in fetches:
        copy.wait()
    lax.fori_loop(0, count, one_slot, 0)


def transform_u_kernel(piece_ref, table_ref, twiddle_ref, out_ref, grid_ref, rows_ref):
    grid_ref[...] = jnp.zeros_like(grid_ref)
    for t in range(GROUPS):
        for slot in range(SLOTS):
            piece = piece_ref[t, 2 * PART * slot : 2 * PART * (slot + 1), :]
            row = piece[0, 0].astype(jnp.int32)
            grid_ref[slot % 2, row] += piece
    cells = [grid_ref[0, r] + grid_ref[1, r] for r in range(TROWS)]
    reached = lax.broadcasted_iota(jnp.int32, (PART, TILE), 1) > 0
    items = [(jnp.where(reached, cell[:PART], 0.0), cell[PART:]) for cell in cells]
    for x1, (a, b) in enumerate(fft(items)):
        c = twiddle_ref[x1, 0:1, :]
        s = twiddle_ref[x1, 1:2, :]
        rows_ref[x1 * PART : (x1 + 1) * PART, :TILE] = a * c - b * s
        rows_ref[x1 * PART : (x1 + 1) * PART, TILE:] = a * s + b * c
    out = dot3(table_ref[0], table_ref[1], rows_ref[...], NT)
    for half in range(2):
        for part in range(2):
            out_ref[pl.ds(2 * half + part, TILE, stride=4), :] = out[
                part * TILE : (part + 1) * TILE, half * TILE : (half + 1) * TILE
            ]


def transform_v_kernel(data_ref, column_ref, twiddle_ref, table_ref, out_ref, rows_ref):
    items = []
    for g in range(GROUPS):
        u = dot3(column_ref[0, g], column_ref[1, g], data_ref[64 * g : 64 * (g + 1), :], NN)
        items.append((u[:COLUMNS], u[COLUMNS:]))
    for ya, (a, b) in enumerate(fft(items)):
        c = twiddle_ref[ya, 0]
        s = twiddle_ref[ya, 1]
        rows_ref[ya * COLUMNS : (ya + 1) * COLUMNS, :TILE] = a * c - b * s
        rows_ref[ya * COLUMNS : (ya + 1) * COLUMNS, TILE:] = a * s + b * c
    out = dot3(table_ref[0], table_ref[1], rows_ref[...], NT)
    for yb in range(PART):
        for half in range(2):
            out_ref[2 * yb + half] = out[
                yb * 16 : (yb + 1) * 16, half * TILE : (half + 1) * TILE
            ]


def phase_factors(plane, x, y):
    along_l = (x - NU // 2).astype(f32) / NU
    along_m = (y - NV // 2).astype(f32) / NV
    height = jnp.sqrt(
        1.0 - along_l[:, None] * along_l[:, None] - along_m[None, :] * along_m[None, :]
    )
    phase = 2.0 * math.pi * plane * (height - 1.0)
    scale = 1.0 / math.sqrt(NU * NV)
    return lax.optimization_barrier((jnp.cos(phase) * scale, jnp.sin(phase) * scale))


VMEM = pl.BlockSpec(memory_space=pltpu.VMEM)
SMEM = pl.BlockSpec(memory_space=pltpu.SMEM)
HBM = pl.BlockSpec(memory_space=pltpu.HBM)


def call(kernel, outs, in_specs, scratch=(), vmem=32):
    return pl.pallas_call(
        kernel,
        out_shape=outs,
        in_specs=in_specs,
        out_specs=VMEM,
        scratch_shapes=list(scratch),
        compiler_params=pltpu.CompilerParams(vmem_limit_bytes=vmem * 1024 * 1024),
    )


def shards(visibilities, coords, tile_row, counts, w_plane):
    def shape(*dims):
        return jax.ShapeDtypeStruct(dims, f32)

    length = 2 * PART * SLOTS
    pieces = call(
        grid_kernel,
        shape(GROUPS, length, TILE),
        [SMEM, HBM, HBM, HBM],
        [
            pltpu.SMEM((1, SLOTS), jnp.int32),
            pltpu.VMEM((SLOTS, 1, 2, BLOCK), f32),
            pltpu.VMEM((SLOTS, 1, 2, BLOCK), f32),
            pltpu.SemaphoreType.DMA(()),
            pltpu.SemaphoreType.DMA((2,)),
        ],
    )(
        counts,
        pltpu.with_memory_space_constraint(tile_row.reshape(1, SLOTS), pltpu.HBM),
        pltpu.with_memory_space_constraint(visibilities, pltpu.HBM),
        pltpu.with_memory_space_constraint(coords, pltpu.HBM),
    )
    pieces = lax.all_to_all(pieces, "tm", 0, 0, tiled=True)
    spectrum = call(
        transform_u_kernel,
        shape(512, TILE),
        [VMEM, VMEM, VMEM],
        [pltpu.VMEM((2, TROWS + 1, 2 * PART, TILE), f32), pltpu.VMEM((256, 256), f32)],
    )(pieces, jnp.asarray(inner_u_table()), jnp.asarray(twiddle_u_table()))
    spectrum = lax.all_to_all(
        spectrum.reshape(256, 2, TILE), ("tm", "col"), 0, 0, tiled=True
    ).reshape(512, TILE)
    image = call(
        transform_v_kernel,
        shape(COLUMNS, 16, TILE),
        [VMEM, VMEM, VMEM, VMEM],
        [pltpu.VMEM((256, 256), f32)],
    )(
        spectrum,
        jnp.asarray(column_table()),
        jnp.asarray(twiddle_v_table()),
        jnp.asarray(inner_v_table()),
    )
    image = lax.all_to_all(image, "col", 0, 0, tiled=True)
    rows = NU // GROUPS
    x = lax.axis_index("tm") * rows + jnp.arange(rows, dtype=jnp.int32)
    y = lax.axis_index("col") * TILE + jnp.arange(TILE, dtype=jnp.int32)
    cosine, sine = phase_factors(w_plane[0], x, y)
    real = image[:, :8, :].reshape(rows, TILE)
    imaginary = image[:, 8:, :].reshape(rows, TILE)
    return real * cosine - imaginary * sine, real * sine + imaginary * cosine


def solution(mesh):
    return jax.shard_map(
        shards,
        mesh=mesh,
        in_specs=(
            P("tm", "col", None, None),
            P("tm", "col", None, None),
            P("tm", "col"),
            P("tm", "col"),
            P(),
        ),
        out_specs=(P("tm", "col"), P("tm", "col")),
        check_vma=False,
    )
```
